256 devices in a mesh: stretch: 64 (over z, x, core), seq: 4 (over y).
Axes of the slice: x: 4, y: 4, z: 8, core: 2. Of those that a mesh axis runs over, the one named last changes fastest.
Arguments:
- queries: bfloat16 [32768, 2560], P(('stretch', 'seq')), may hold values from -32 to 32
- keys: bfloat16 [32768, 2560], P(('stretch', 'seq')), may hold values from -32 to 32
- values: bfloat16 [32768, 2560], P(('stretch', 'seq')), may hold values from -6 to 6
- q_gain: float32 [2560], replicated, may hold values from 0.1 to 1.9
- k_gain: float32 [2560], replicated, may hold values from 0.1 to 1.9
- out_weight: bfloat16 [2560, 5120], P('seq'), may hold values from -0.125 to 0.125
- gate_table: bfloat16 [50, 5120], replicated, may hold values from -96 to 96
- noise_level: int32 [64], P('stretch'), may hold values from 0 to 49
- first_stretch: int32 [64], P('stretch'), may hold values from 0 to 62, as said below
Outputs:
- mixed: bfloat16 [32768, 5120], P(('stretch', 'seq'))
The draws below stay inside these ranges and needn't reach their ends.
Inputs may be any that keep to these rules, and one draw needn't show every extreme that they name: first_stretch[c] lies between max(c - 7, 0) and c; the last stretch attends to two or more stretches; in every draw some stretch attends to exactly 8 stretches.
All inputs are finite; a program needn't handle non-finite values.
Results may differ from the reference program's by a relative error of at most 0.018.
Values may be sent and summed in bfloat16 or wider, within the bound.
No kernel may reach another device: no remote copies, remote signals or barrier semaphores. Data moves between devices by JAX's collectives and lax.ppermute only.
A program may use at most 128 MiB of HBM per device.

```python
import jax
import jax.numpy as jnp
from jax import lax

D = 5120
HEADS = 20
HS = 128
L = 512
LEVELS = 50
WINDOW = 8
HD = 2560
STRETCHES = 64
TOKENS = 32768


def draw_queries(key, part):
    key = jax.random.fold_in(key, 1)
    own_part = jnp.clip(jax.random.normal(key, (TOKENS, HD), jnp.float32), -4.0, 4.0)
    return own_part.astype(jnp.bfloat16)


def draw_keys(key, part):
    key = jax.random.fold_in(key, 2)
    own_part = jnp.clip(jax.random.normal(key, (TOKENS, HD), jnp.float32), -4.0, 4.0)
    return own_part.astype(jnp.bfloat16)


def draw_first_stretch(key, part):
    key = jax.random.fold_in(key, 3)
    span_key, pick_key = jax.random.split(key)
    spans = jax.random.randint(span_key, (STRETCHES,), 0, WINDOW)
    picked = jax.random.randint(pick_key, (), WINDOW - 1, STRETCHES)
    stretch_ids = jnp.arange(STRETCHES)
    last_id = STRETCHES - 1
    spans = jnp.where(stretch_ids == last_id, jnp.maximum(spans, 1), spans)
    spans = jnp.where((stretch_ids == last_id - 1) & (picked != last_id - 1), 0, spans)
    spans = jnp.where((stretch_ids == last_id) & (picked == last_id - 1), 1, spans)
    spans = jnp.where(stretch_ids == picked, WINDOW - 1, spans)
    return jnp.maximum(stretch_ids - spans, 0).astype(jnp.int32)


def with_ends(entries, own_key, smallest, largest):
    longest = entries.shape.index(max(entries.shape))
    spots = []
    for shift in (0, 1):
        where = [jax.random.randint(jax.random.fold_in(own_key, axis), (), 0, length) for axis, length in enumerate(entries.shape)]
        where[longest] = (where[longest] + shift) % entries.shape[longest]
        spots.append(tuple(where))
    return entries.at[spots[0]].set(smallest).at[spots[1]].set(largest)


def levels(key, dims, pieces, least, top_value):
    gain, own = 1.0, jax.random.fold_in(key, 6)
    for axis_at, shards_of in pieces:
        heights = jnp.exp(jax.random.uniform(jax.random.fold_in(own, axis_at), (shards_of,), jnp.float32, least / len(pieces), top_value / len(pieces)))
        gain = gain * jnp.repeat(heights, dims[axis_at] // shards_of).reshape([-1 if axis == axis_at else 1 for axis in range(len(dims))])
    return gain


def normal_values(key, shape, scale, limit, cuts=(), kind=jnp.bfloat16):
    gain = levels(key, shape, cuts, -0.22, 0.18) if cuts else 1.0
    drawn = jax.random.normal(key, shape, jnp.float32) * scale * gain
    return jnp.minimum(jnp.maximum(drawn, -limit), limit).astype(kind)


def setup_inputs(seed: int = 0) -> dict:
    key_of = jax.random.split(jax.random.key(seed), 10)
    return {
        "queries": draw_queries(jax.random.fold_in(key_of[9], 71), 0),
        "keys": draw_keys(jax.random.fold_in(key_of[9], 71), 0),
        "values": normal_values(key_of[2], (TOKENS, HD), 1.0, 6.0, ((0, 256),)),
        "q_gain": jnp.clip(1.0 + 0.18 * jax.random.normal(key_of[3], (HD,), jnp.float32), 0.1, 1.9),
        "k_gain": jnp.clip(1.0 + 0.18 * jax.random.normal(key_of[4], (HD,), jnp.float32), 0.1, 1.9),
        "out_weight": normal_values(key_of[5], (HD, D), HD ** -0.5, 0.125, ((0, 4),)),
        "gate_table": normal_values(key_of[6], (LEVELS, D), 16.0, 96.0),
        "noise_level": with_ends(jax.random.randint(key_of[7], (STRETCHES,), 0, LEVELS), jax.random.fold_in(key_of[7], 1), 0, LEVELS - 1).astype(jnp.int32),
        "first_stretch": draw_first_stretch(jax.random.fold_in(key_of[9], 71), 0),
    }


def normed(values_in, gain_vec):
    widened = values_in.astype(jnp.float32)
    mean_square = lax.optimization_barrier(jnp.mean(widened * widened, axis=-1, keepdims=True))
    return (widened * lax.rsqrt(mean_square + 1e-06) * gain_vec).astype(jnp.bfloat16)

def reference(queries, keys, values, q_gain, k_gain, out_weight, gate_table, noise_level, first_stretch):
    q_heads = normed(queries, q_gain).reshape(STRETCHES, L, HEADS, HS)
    k_heads = normed(keys, k_gain).reshape(STRETCHES, L, HEADS, HS)
    v_heads = values.reshape(STRETCHES, L, HEADS, HS)
    score_scale = 1.0 / HS ** 0.5

    def per_stretch(stretch_id):
        offsets = jnp.arange(WINDOW, dtype=jnp.int32)
        stretch_ids = stretch_id - offsets
        is_active = stretch_ids >= first_stretch[stretch_id]
        stretch_ids = jnp.maximum(stretch_ids, 0).astype(jnp.int32)
        key_window = k_heads[stretch_ids].astype(jnp.float32)
        value_window = v_heads[stretch_ids].astype(jnp.float32)
        query = lax.dynamic_index_in_dim(q_heads, stretch_id, 0, keepdims=False).astype(jnp.float32)
        scores = jnp.einsum('qhd,wkhd->hqwk', query, key_window) * score_scale
        mask = is_active[None, None, :, None]
        scores = jnp.where(mask, scores, -1e+30)
        row_max = lax.optimization_barrier(jnp.max(scores, axis=(2, 3), keepdims=True))
        weights = jnp.where(mask, jnp.exp(scores - row_max), 0.0)
        denom = lax.optimization_barrier(jnp.sum(weights, axis=(2, 3)))
        rounded = weights.astype(jnp.bfloat16).astype(jnp.float32)
        summed = jnp.einsum('hqwk,wkhd->qhd', rounded, value_window)
        attended = (summed / denom.T[:, :, None]).reshape(L, HD).astype(jnp.bfloat16)
        projected = jnp.dot(attended, out_weight, preferred_element_type=jnp.float32)
        gate_row = gate_table[noise_level[stretch_id]].astype(jnp.float32)
        return (projected * gate_row[None, :]).astype(jnp.bfloat16)
    mixed = lax.map(per_stretch, jnp.arange(STRETCHES, dtype=jnp.int32))
    return mixed.reshape(TOKENS, D)
```

```python
import functools

import jax
import jax.numpy as jnp
from jax import lax
from jax.experimental import pallas as pl
from jax.experimental.pallas import tpu as pltpu
from jax.sharding import PartitionSpec as P

HS = 128
WINDOW = 8
LOG2E = 1.4426950408889634
CHUNKS = ((0, 2), (2, 5))
NEAR, FAR = 2.0**-60, 2.0**100
VMEM_BYTES = 48 * 2**20


def prep_kv_kernel(groups, keys_ref, values_ref, gain_ref, *out_refs):
    wide = keys_ref[...].astype(jnp.float32)
    mean_square = jnp.mean(wide * wide, axis=-1, keepdims=True)
    normed = (wide * lax.rsqrt(mean_square + 1e-06) * gain_ref[...]).astype(jnp.bfloat16)
    share = normed.shape[1] // groups
    for (low, high), out_ref in zip(CHUNKS, out_refs):
        for dest in range(groups):
            cols = slice(dest * share + low * HS, dest * share + high * HS)
            out_ref[dest, 0] = normed[:, cols]
            out_ref[dest, 1] = values_ref[:, cols]


def prep_q_kernel(groups, queries_ref, gain_ref, out_ref):
    wide = queries_ref[...].astype(jnp.float32)
    mean_square = jnp.mean(wide * wide, axis=-1, keepdims=True)
    scaled_gain = gain_ref[...] * (LOG2E / HS**0.5)
    normed = (wide * lax.rsqrt(mean_square + 1e-06) * scaled_gain).astype(jnp.bfloat16)
    share = normed.shape[1] // groups
    for dest in range(groups):
        out_ref[dest] = normed[:, dest * share : (dest + 1) * share]


def attend_kernel(active_ref, q_ref, *refs):
    slots, (out_ref, acc_ref, max_ref) = refs[:WINDOW], refs[WINDOW:]
    length = out_ref.shape[0]
    ones = jnp.ones((length, HS), jnp.bfloat16)
    query = q_ref[...].reshape(length, HS)

    def key_and_value(index):
        key = slots[index][:, 0].reshape(length, HS)
        value = jnp.concatenate([slots[index][:, 1].reshape(length, HS), ones], axis=1)
        return key, value

    def scores_of(key):
        return lax.dot_general(
            query, key, (((1,), (1,)), ((), ())), preferred_element_type=jnp.float32
        )

    def times_value(weights, value):
        return jnp.dot(weights.astype(jnp.bfloat16), value, preferred_element_type=jnp.float32)

    for index in range(WINDOW):
        key, value = key_and_value(index)
        if index:
            flag = active_ref[index].astype(jnp.float32).astype(jnp.bfloat16)
            key, value = key * flag, value * flag
        part = times_value(jnp.exp2(scores_of(key)), value)
        if index:
            acc_ref[...] += part
        else:
            acc_ref[...] = part
    total = acc_ref[:, HS:]
    in_range = (jnp.min(total) > NEAR) & (jnp.max(total) < FAR)

    @pl.when(jnp.logical_not(in_range))
    def _():
        for index in range(WINDOW):

            @pl.when(active_ref[index] != 0)
            def _():
                key, value = key_and_value(index)
                scores = scores_of(key)
                new_max = jnp.max(scores, axis=1, keepdims=True)
                if index:
                    old_max = max_ref[...]
                    new_max = jnp.maximum(old_max, new_max)
                part = times_value(jnp.exp2(scores - new_max), value)
                if index:
                    part = acc_ref[...] * jnp.exp2(old_max - new_max) + part
                max_ref[...] = new_max
                acc_ref[...] = part

    out_ref[...] = (acc_ref[:, :HS] / acc_ref[:, HS:]).astype(jnp.bfloat16)


def attend(active, query, slots, low, high):
    groups, rows, _ = query.shape
    length, heads = groups * rows, high - low
    grid_spec = pltpu.PrefetchScalarGridSpec(
        num_scalar_prefetch=1,
        grid=(heads,),
        in_specs=[pl.BlockSpec((groups, rows, HS), lambda head, _: (0, 0, low + head))]
        + [pl.BlockSpec((groups, 2, rows, HS), lambda head, _: (0, 0, 0, head))] * WINDOW,
        out_specs=pl.BlockSpec((length, HS), lambda head, _: (0, head)),
        scratch_shapes=[
            pltpu.VMEM((length, 2 * HS), jnp.float32),
            pltpu.VMEM((length, 1), jnp.float32),
        ],
    )
    flops = heads * WINDOW * length * length * HS * 8
    return pl.pallas_call(
        attend_kernel,
        grid_spec=grid_spec,
        out_shape=jax.ShapeDtypeStruct((length, heads * HS), jnp.bfloat16),
        compiler_params=pltpu.CompilerParams(vmem_limit_bytes=VMEM_BYTES),
        cost_estimate=pl.CostEstimate(
            flops=flops, bytes_accessed=20 * length * heads * HS * 2, transcendentals=0
        ),
        name="attend",
    )(active, query, *slots)


def project_kernel(count, places_ref, gate_ref, *refs):
    parts, (near_ref, far_ref, out_ref) = refs[:-3], refs[-3:]
    step = pl.program_id(0)

    def run(weight_ref):
        total = None
        for d in range(count):
            for c, (low, high) in enumerate(CHUNKS):
                term = jnp.dot(
                    parts[d * len(CHUNKS) + c][...],
                    weight_ref[d, low * HS : high * HS, :],
                    preferred_element_type=jnp.float32,
                )
                total = term if total is None else total + term
        out_ref[...] = (total * gate_ref[...]).astype(jnp.bfloat16).reshape(out_ref.shape)

    @pl.when(step == 0)
    def _():
        run(near_ref)

    @pl.when(step == 1)
    def _():
        run(far_ref)


def project(places, gate_row, parts, near, far):
    count, _, width = near.shape
    length = parts[0].shape[0]
    whole = lambda array: pl.BlockSpec(array.shape, lambda step, _: (0,) * array.ndim)
    grid_spec = pltpu.PrefetchScalarGridSpec(
        num_scalar_prefetch=1,
        grid=(2,),
        in_specs=[pl.BlockSpec((1, width), lambda step, places: (0, places[step]))]
        + [whole(array) for array in (*parts, near, far)],
        out_specs=pl.BlockSpec(
            (count, length // count, width), lambda step, places: (0, 0, places[step])
        ),
    )
    return pl.pallas_call(
        functools.partial(project_kernel, count),
        grid_spec=grid_spec,
        out_shape=jax.ShapeDtypeStruct((count, length // count, 2 * width), jnp.bfloat16),
        compiler_params=pltpu.CompilerParams(vmem_limit_bytes=VMEM_BYTES),
        cost_estimate=pl.CostEstimate(
            flops=4 * length * near.size, bytes_accessed=4 * near.size, transcendentals=0
        ),
        name="project",
    )(places, gate_row, *parts, near, far)


def shards(
    queries, keys, values, q_gain, k_gain, out_weight, gate_table, noise_level, first_stretch
):
    groups = lax.axis_size("seq")
    rows, feats = queries.shape
    share = feats // groups
    spot = lax.axis_index("stretch")
    place = lax.axis_index("seq")
    core, x_at = spot % 2, (spot // 2) % 4

    chips = lax.axis_size("stretch") // 2

    def chip_step(steps):
        return [
            (2 * chip + c, 2 * ((chip + steps) % chips) + c)
            for chip in range(chips)
            for c in range(2)
        ]

    def row_step(steps):
        return [
            (2 * chip + c, 2 * (chip // 4 * 4 + (chip + steps) % 4) + c)
            for chip in range(chips)
            for c in range(2)
        ]

    along = lambda value, pairs: lax.ppermute(value, "stretch", pairs)
    swap = lambda value: along(value, [(i, i ^ 1) for i in range(2 * chips)])
    turn = lambda value, d: (
        lax.ppermute(value, "seq", [(i, (i + d) % groups) for i in range(groups)]) if d else value
    )

    kv_chunks = pl.pallas_call(
        functools.partial(prep_kv_kernel, groups),
        out_shape=[
            jax.ShapeDtypeStruct((groups, 2, rows, (high - low) * HS), jnp.bfloat16)
            for low, high in CHUNKS
        ],
        name="prep_kv",
    )(keys, values, k_gain[None])
    q_parts = pl.pallas_call(
        functools.partial(prep_q_kernel, groups),
        out_shape=jax.ShapeDtypeStruct((groups, rows, share), jnp.bfloat16),
        name="prep_q",
    )(queries, q_gain[None])

    own_chunks = [lax.all_to_all(chunk, "seq", 0, 0) for chunk in kv_chunks]
    query = lax.all_to_all(q_parts, "seq", 0, 0)

    turns = (0, 1, -1, 2)
    width = out_weight.shape[1] // groups
    half = width // 2
    near = jnp.stack(
        [
            turn(
                lax.dynamic_slice_in_dim(
                    out_weight, (place + d) % groups * width + core * half, half, 1
                ),
                d,
            )
            for d in turns
        ]
    )
    far = swap(near)

    offsets = jnp.where(
        core == 0,
        jnp.array((0, 7, 2, 1, 6, 5, 4, 3), jnp.int32),
        jnp.array((0, 1, 2, 3, 6, 7, 4, 5), jnp.int32),
    )
    active = (offsets <= spot - first_stretch[0]).astype(jnp.int32)

    parts = [[] for _ in turns]
    for (low, high), own in zip(CHUNKS, own_chunks):
        shifted = along(own, chip_step(4))
        one = along(jnp.where(x_at < 3, own, shifted), row_step(1))
        three = along(jnp.where(x_at > 0, shifted, own), row_step(-1))
        pair = swap(jnp.where(core == 0, own, shifted))
        two = jnp.concatenate(
            [along(one[: groups // 2], chip_step(1)), along(three[groups // 2 :], chip_step(-1))]
        )
        slots = (own, pair, one, swap(one), three, swap(three), two, swap(two))
        attended = attend(active, query, slots, low, high)
        for index, d in enumerate(turns):
            parts[index].append(turn(attended, d))

    gate_row = lax.dynamic_slice(
        gate_table, (noise_level[0], place * width), (1, width)
    ).astype(jnp.float32)
    places = jnp.stack([core, 1 - core]).astype(jnp.int32)
    mixed = project(places, gate_row, [part for group in parts for part in group], near, far)
    mixed = lax.all_to_all(mixed, "seq", 0, 0)
    return jnp.swapaxes(mixed, 0, 1).reshape(rows, groups * width)


def solution(mesh):
    return jax.shard_map(
        shards,
        mesh=mesh,
        in_specs=(
            P(("stretch", "seq"), None),
            P(("stretch", "seq"), None),
            P(("stretch", "seq"), None),
            P(),
            P(),
            P("seq", None),
            P(),
            P("stretch"),
            P("stretch"),
        ),
        out_specs=P(("stretch", "seq"), None),
        check_vma=False,
    )
```

```python
import functools

import jax
import jax.numpy as jnp
from jax import lax
from jax.experimental import pallas as pl
from jax.experimental.pallas import tpu as pltpu
from jax.sharding import PartitionSpec as P

HS = 128
WINDOW = 8
LOG2E = 1.4426950408889634
CHUNKS = ((0, 1), (1, 3), (3, 5))
TURNS = (0, 1, -1, 2)
NEAR, FAR = 2.0**-60, 2.0**100
VMEM_BYTES = 62 * 2**20


def prep_kv_kernel(groups, place_ref, keys_ref, values_ref, gain_ref, *refs):
    out_refs, normed_ref = refs[:-1], refs[-1]
    wide = keys_ref[...].astype(jnp.float32)
    mean_square = jnp.mean(wide * wide, axis=-1, keepdims=True)
    normed_ref[...] = (wide * lax.rsqrt(mean_square + 1e-06) * gain_ref[...][None, :]).astype(jnp.bfloat16)
    share = wide.shape[1] // groups
    low, high = CHUNKS[0]
    for d, out_ref in zip(TURNS, out_refs):
        start = (place_ref[0] + d + groups) % groups * share + low * HS
        cols = pl.ds(pl.multiple_of(start, HS), (high - low) * HS)
        out_ref[0] = normed_ref[:, cols]
        out_ref[1] = values_ref[:, cols]
    for c, (low, high) in enumerate(CHUNKS[1:]):
        for dest in range(groups):
            cols = slice(dest * share + low * HS, dest * share + high * HS)
            out_refs[-1][dest, c, 0] = normed_ref[:, cols]
            out_refs[-1][dest, c, 1] = values_ref[:, cols]


def pack_kernel(core_ref, weight_ref, out_ref):
    out_ref[0] = weight_ref[...]


def pack(core, weight, groups):
    depth, width = weight.shape
    half = width // groups // 2
    return pl.pallas_call(
        pack_kernel,
        grid_spec=pltpu.PrefetchScalarGridSpec(
            num_scalar_prefetch=1,
            grid=(groups,),
            in_specs=[pl.BlockSpec((depth, half), lambda dest, core: (0, 2 * dest + core[0]))],
            out_specs=pl.BlockSpec((1, depth, half), lambda dest, core: (dest, 0, 0)),
        ),
        out_shape=jax.ShapeDtypeStruct((groups, depth, half), weight.dtype),
        name="pack",
    )(core, weight)


def prep_q_kernel(groups, queries_ref, gain_ref, out_ref):
    wide = queries_ref[...].astype(jnp.float32)
    mean_square = jnp.mean(wide * wide, axis=-1, keepdims=True)
    scaled_gain = gain_ref[...][None, :] * (LOG2E / HS**0.5)
    normed = (wide * lax.rsqrt(mean_square + 1e-06) * scaled_gain).astype(jnp.bfloat16)
    share = normed.shape[1] // groups
    for dest in range(groups):
        out_ref[dest] = normed[:, dest * share : (dest + 1) * share]


def attend_kernel(active_ref, q_ref, *refs):
    slots, (out_ref, acc_ref, max_ref) = refs[:WINDOW], refs[WINDOW:]
    length = out_ref.shape[0]
    ones = jnp.ones((length, HS), jnp.bfloat16)

    def key_of(index):
        return slots[index][:, 0].reshape(length, HS)

    def value_of(index):
        return jnp.concatenate([slots[index][:, 1].reshape(length, HS), ones], axis=1)

    def scores_of(query, index):
        return lax.dot_general(
            query, key_of(index), (((1,), (1,)), ((), ())), preferred_element_type=jnp.float32
        )

    def times_value(weights, index):
        return jnp.dot(
            weights.astype(jnp.bfloat16), value_of(index), preferred_element_type=jnp.float32
        )

    total = None
    for index in range(WINDOW):
        scores = scores_of(q_ref[...], index)
        if index:
            scores = scores + jnp.where(active_ref[index] != 0, 0.0, -1e30)
        part = times_value(jnp.exp2(scores), index)
        total = part if total is None else total + part
    acc_ref[...] = total
    denom = total[:, HS:]
    in_range = (jnp.min(denom) > NEAR) & (jnp.max(denom) < FAR)

    @pl.when(jnp.logical_not(in_range))
    def _():
        def redo(block, _):
            rows = pl.ds(pl.multiple_of(block * HS, HS), HS)
            query = q_ref[rows, :]
            for index in range(WINDOW):

                @pl.when(active_ref[index] != 0)
                def _():
                    scores = scores_of(query, index)
                    new_max = jnp.max(scores, axis=1, keepdims=True)
                    if index:
                        old_max = max_ref[...]
                        new_max = jnp.maximum(old_max, new_max)
                    part = times_value(jnp.exp2(scores - new_max), index)
                    if index:
                        part = acc_ref[rows, :] * jnp.exp2(old_max - new_max) + part
                    max_ref[...] = new_max
                    acc_ref[rows, :] = part

            return 0

        lax.fori_loop(0, length // HS, redo, 0)

    out_ref[...] = (acc_ref[:, :HS] / acc_ref[:, HS:]).astype(jnp.bfloat16)


def attend(active, query, slots, low, high):
    length, heads = query.shape[0], high - low
    groups, _, rows, _ = slots[0].shape
    grid_spec = pltpu.PrefetchScalarGridSpec(
        num_scalar_prefetch=1,
        grid=(heads,),
        in_specs=[pl.BlockSpec((length, HS), lambda head, _: (0, low + head))]
        + [pl.BlockSpec((groups, 2, rows, HS), lambda head, _: (0, 0, 0, head))] * WINDOW,
        out_specs=pl.BlockSpec((length, HS), lambda head, _: (0, head)),
        scratch_shapes=[
            pltpu.VMEM((length, 2 * HS), jnp.float32),
            pltpu.VMEM((HS, 1), jnp.float32),
        ],
    )
    flops = heads * WINDOW * length * length * HS * 8
    return pl.pallas_call(
        attend_kernel,
        grid_spec=grid_spec,
        out_shape=jax.ShapeDtypeStruct((length, heads * HS), jnp.bfloat16),
        compiler_params=pltpu.CompilerParams(vmem_limit_bytes=VMEM_BYTES),
        cost_estimate=pl.CostEstimate(
            flops=flops, bytes_accessed=20 * length * heads * HS * 2, transcendentals=0
        ),
        name="attend",
    )(active, query, *slots)


def part_copies(parts, held_ref, sems):
    depth = parts[0].shape[1]
    return [
        pltpu.make_async_copy(
            part, held_ref.at[:, pl.ds(index * depth, depth)], sems.at[index]
        )
        for index, part in enumerate(parts)
    ]


def weight_copies(place, weight_ref, span, held_ref, sems):
    count = len(TURNS)
    depth = (span[1] - span[0]) * HS
    return [
        pltpu.make_async_copy(
            weight_ref.at[(place - d + count) % count, pl.ds(span[0] * HS, depth), :],
            held_ref.at[pl.ds(index * depth, depth), :],
            sems.at[index],
        )
        for index, d in enumerate(TURNS)
    ]


def product(left, right):
    return jnp.dot(left[...], right[...], preferred_element_type=jnp.float32)


def project_early_kernel(span, place_ref, *refs):
    parts, refs = refs[: len(TURNS)], refs[len(TURNS) :]
    near_ref, far_ref, near_out, far_out, left, near_held, far_held, sems = refs
    first = part_copies(parts, left, sems.at[0])
    first += weight_copies(place_ref[0], near_ref, span, near_held, sems.at[1])
    second = weight_copies(place_ref[0], far_ref, span, far_held, sems.at[2])
    for copy in first + second:
        copy.start()
    for copy in first:
        copy.wait()
    near_out[...] = product(left, near_held)
    for copy in second:
        copy.wait()
    far_out[...] = product(left, far_held)


def project_early(place, parts, near, far, span):
    length, width = parts[0].shape[0], near.shape[2]
    depth = (span[1] - span[0]) * HS
    shape = jax.ShapeDtypeStruct((length, width), jnp.float32)
    smem = pl.BlockSpec(memory_space=pltpu.SMEM)
    return pl.pallas_call(
        functools.partial(project_early_kernel, span),
        in_specs=[smem] + [pl.BlockSpec(memory_space=pl.ANY)] * (len(parts) + 2),
        out_shape=(shape, shape),
        scratch_shapes=[
            pltpu.VMEM((length, len(TURNS) * depth), jnp.bfloat16),
            pltpu.VMEM((len(TURNS) * depth, width), jnp.bfloat16),
            pltpu.VMEM((len(TURNS) * depth, width), jnp.bfloat16),
            pltpu.SemaphoreType.DMA((3, len(TURNS))),
        ],
        compiler_params=pltpu.CompilerParams(vmem_limit_bytes=VMEM_BYTES),
        cost_estimate=pl.CostEstimate(
            flops=2 * length * near.size, bytes_accessed=4 * near.size, transcendentals=0
        ),
        name="project_early",
    )(place, *parts, near, far)


def project_late_kernel(span, place_ref, gate_ref, early_ref, *refs):
    count = len(TURNS)
    parts, weight_ref = refs[:count], refs[count]
    out_refs, (whole_ref, left, held_ref, sems) = refs[count + 1 : -4], refs[-4:]
    copies = part_copies(parts, left, sems.at[0])
    copies += weight_copies(place_ref[0], weight_ref, span, held_ref, sems.at[1])
    for copy in copies:
        copy.start()
    for copy in copies:
        copy.wait()
    total = early_ref[...] + product(left, held_ref)
    whole_ref[...] = (total * gate_ref[...]).astype(jnp.bfloat16)
    rows = whole_ref.shape[0] // count
    for d, out_ref in zip(TURNS, out_refs):
        start = pl.multiple_of((place_ref[0] + d + count) % count * rows, rows)
        out_ref[...] = whole_ref[pl.ds(start, rows), :]


def project_late(place, gate_row, early, parts, weight, span):
    length, width = early.shape
    depth = (span[1] - span[0]) * HS
    smem, vmem = pl.BlockSpec(memory_space=pltpu.SMEM), pl.BlockSpec(memory_space=pltpu.VMEM)
    return pl.pallas_call(
        functools.partial(project_late_kernel, span),
        in_specs=[smem, vmem, vmem] + [pl.BlockSpec(memory_space=pl.ANY)] * (len(parts) + 1),
        out_shape=[jax.ShapeDtypeStruct((length // len(TURNS), width), jnp.bfloat16)] * len(TURNS),
        scratch_shapes=[
            pltpu.VMEM((length, width), jnp.bfloat16),
            pltpu.VMEM((length, len(TURNS) * depth), jnp.bfloat16),
            pltpu.VMEM((len(TURNS) * depth, width), jnp.bfloat16),
            pltpu.SemaphoreType.DMA((2, len(TURNS))),
        ],
        compiler_params=pltpu.CompilerParams(vmem_limit_bytes=VMEM_BYTES),
        cost_estimate=pl.CostEstimate(
            flops=length * weight.size, bytes_accessed=2 * weight.size, transcendentals=0
        ),
        name="project_late",
    )(place, gate_row, early, *parts, weight)


def assemble_kernel(place_ref, core_ref, *refs):
    parts, out_ref = refs[:-1], refs[-1]
    count = len(TURNS)
    half = parts[0].shape[1]
    for index, part in enumerate(parts):
        source = (place_ref[0] - TURNS[index % count] + count) % count
        side = core_ref[0] if index < count else 1 - core_ref[0]
        start = pl.multiple_of((2 * source + side) * half, HS)
        out_ref[:, pl.ds(start, half)] = part[...]


def assemble(place, core, parts):
    rows, half = parts[0].shape
    smem, vmem = pl.BlockSpec(memory_space=pltpu.SMEM), pl.BlockSpec(memory_space=pltpu.VMEM)
    return pl.pallas_call(
        assemble_kernel,
        in_specs=[smem, smem] + [vmem] * len(parts),
        out_shape=jax.ShapeDtypeStruct((rows, half * len(parts)), jnp.bfloat16),
        name="assemble",
    )(place, core, *parts)


def shards(
    queries, keys, values, q_gain, k_gain, out_weight, gate_table, noise_level, first_stretch
):
    groups = lax.axis_size("seq")
    rows, feats = queries.shape
    share = feats // groups
    spot = lax.axis_index("stretch")
    place = lax.axis_index("seq")
    core, x_at = spot % 2, (spot // 2) % 4

    chips = lax.axis_size("stretch") // 2

    def chip_step(steps):
        return [
            (2 * chip + c, 2 * ((chip + steps) % chips) + c)
            for chip in range(chips)
            for c in range(2)
        ]

    def row_step(steps):
        return [
            (2 * chip + c, 2 * (chip // 4 * 4 + (chip + steps) % 4) + c)
            for chip in range(chips)
            for c in range(2)
        ]

    def along(value, pairs, label):
        with jax.named_scope(label):
            return lax.ppermute(value, "stretch", pairs)

    def swap(value, label):
        return along(value, [(i, i ^ 1) for i in range(2 * chips)], "swap_" + label)

    def turn(value, d, label):
        if not d:
            return value
        with jax.named_scope(f"{label}_turn_{d % groups}"):
            return lax.ppermute(value, "seq", [(i, (i + d) % groups) for i in range(groups)])


    place_word = place[None].astype(jnp.int32)
    core_word = core[None].astype(jnp.int32)
    sizes = [(high - low) * HS for low, high in CHUNKS]
    kv_shapes = [jax.ShapeDtypeStruct((2, rows, sizes[0]), jnp.bfloat16) for _ in TURNS] + [
        jax.ShapeDtypeStruct((groups, 2, 2, rows, sizes[1]), jnp.bfloat16)
    ]
    smem, vmem = pl.BlockSpec(memory_space=pltpu.SMEM), pl.BlockSpec(memory_space=pltpu.VMEM)
    kv_pieces = pl.pallas_call(
        functools.partial(prep_kv_kernel, groups),
        in_specs=[smem, vmem, vmem, vmem],
        out_shape=kv_shapes,
        scratch_shapes=[pltpu.VMEM((rows, feats), jnp.bfloat16)],
        name="prep_kv",
    )(place_word, keys, values, k_gain)
    count = len(TURNS)
    width = out_weight.shape[1] // groups
    half = width // 2

    def after(done, *waiting):
        return lax.optimization_barrier((done, waiting))[1]

    def shift(own, c):
        return along(own, chip_step(4), f"shift{c}")

    def row_pair(own, shifted):
        return jnp.where(x_at < 3, own, shifted), jnp.where(x_at > 0, shifted, own)

    def core_pair(own, shifted):
        return jnp.where(core == 0, own, shifted)

    offsets = jnp.where(
        core == 0,
        jnp.array((0, 7, 2, 1, 6, 5, 4, 3), jnp.int32),
        jnp.array((0, 1, 2, 3, 6, 7, 4, 5), jnp.int32),
    )
    active = (offsets <= spot - first_stretch[0]).astype(jnp.int32)

    first_pieces = [turn(piece, d, "kv0") for piece, d in zip(kv_pieces[:count], TURNS)]
    q_parts = pl.pallas_call(
        functools.partial(prep_q_kernel, groups),
        out_shape=jax.ShapeDtypeStruct((groups, rows, share), jnp.bfloat16),
        name="prep_q",
    )(queries, q_gain)

    first_pieces, q_parts = after(q_parts, first_pieces, q_parts)
    own0 = jnp.stack(first_pieces)
    (rest,) = after(own0, kv_pieces[-1])
    packed = pack(core_word, out_weight, groups)
    shift0, packed = after(packed, shift(own0, 0), packed)
    rest = lax.all_to_all(rest, "seq", 0, 0)

    right0, left0 = row_pair(own0, shift0)
    one0, three0 = along(right0, row_step(1), "one0"), along(left0, row_step(-1), "three0")
    pair0 = swap(core_pair(own0, shift0), "pair0")
    (rest,) = after(pair0, rest)
    own1, own2 = rest[:, 0], rest[:, 1]
    shift1 = shift(own1, 1)
    q_parts, own2 = after(own1, q_parts, own2)
    two0 = along(one0, chip_step(1), "two0")
    query = lax.all_to_all(q_parts, "seq", 0, 0).reshape(groups * rows, share)

    shift1, own2 = after((one0, three0, shift1), shift1, own2)
    right1, left1 = row_pair(own1, shift1)
    one1, three1 = along(right1, row_step(1), "one1"), along(left1, row_step(-1), "three1")
    shift2 = shift(own2, 2)
    pair1 = swap(core_pair(own1, shift1), "pair1")
    (packed,) = after((one1, three1, shift2, two0), packed)
    near = lax.all_to_all(packed, "seq", 0, 0)

    own2, shift2, next_three1 = after((one1, three1, shift2, pair1), own2, shift2, three1)
    right2, left2 = row_pair(own2, shift2)
    one2 = along(right2, row_step(1), "one2")
    two1 = along(next_three1, chip_step(-1), "two1")
    one0s, three0s = swap(one0, "one0"), swap(three0, "three0")
    two0s = swap(two0, "two0")
    pair2 = swap(core_pair(own2, shift2), "pair2")

    slots = (own0, pair0, one0, one0s, three0, three0s, two0, two0s)
    attended0 = attend(active, query, slots, *CHUNKS[0])

    done = (one2, two1, pair2, attended0)
    left2, next_one2, next_one1, next_three1, next_two1, attended0 = after(
        done, left2, one2, one1, three1, two1, attended0
    )
    three2 = along(left2, row_step(-1), "three2")
    two2 = along(next_one2, chip_step(1), "two2")
    one1s, three1s = swap(next_one1, "one1"), swap(next_three1, "three1")
    two1s = swap(next_two1, "two1")
    slots = (own1, pair1, one1, one1s, three1, three1s, two1, two1s)
    attended1 = attend(active, query, slots, *CHUNKS[1])

    done = (three2, two2, attended1)
    next_one2, next_three2, next_two2, near = after(done, one2, three2, two2, near)
    one2s, three2s = swap(next_one2, "one2"), swap(next_three2, "three2")
    two2s = swap(next_two2, "two2")
    attended01 = jnp.concatenate([attended0, attended1], axis=1)
    gathered01 = [turn(attended01, d, "attended01") for d in TURNS]
    far = swap(near, "weight")
    slots = (own2, pair2, one2, one2s, three2, three2s, two2, two2s)
    attended2 = attend(active, query, slots, *CHUNKS[2])
    gathered2 = [turn(attended2, d, "attended2") for d in TURNS]

    early_span, late_span = (0, CHUNKS[-1][0]), CHUNKS[-1]
    gate_row = lax.dynamic_slice(
        gate_table, (noise_level[0], place * width), (1, width)
    ).astype(jnp.float32)
    mixed = []
    for weight, early, side in zip(
        (near, far), project_early(place_word, gathered01, near, far, early_span), (core, 1 - core)
    ):
        gate_half = lax.dynamic_slice_in_dim(gate_row, side * half, half, 1)
        pieces = project_late(place_word, gate_half, early, gathered2, weight, late_span)
        mixed += [turn(piece, d, "mixed") for piece, d in zip(pieces, TURNS)]
    return assemble(place_word, core_word, mixed)


def solution(mesh):
    return jax.shard_map(
        shards,
        mesh=mesh,
        in_specs=(
            P(("stretch", "seq"), None),
            P(("stretch", "seq"), None),
            P(("stretch", "seq"), None),
            P(),
            P(),
            P("seq", None),
            P(),
            P("stretch"),
            P("stretch"),
        ),
        out_specs=P(("stretch", "seq"), None),
        check_vma=False,
    )
```

```python
import functools

import jax
import jax.numpy as jnp
from jax import lax
from jax.experimental import pallas as pl
from jax.experimental.pallas import tpu as pltpu
from jax.sharding import PartitionSpec as P

HS = 128
WINDOW = 8
LOG2E = 1.4426950408889634
CHUNKS = ((0, 3), (3, 5))
TURNS = (0, 1, -1, 2)
NEAR, FAR = 2.0**-60, 2.0**100
VMEM_BYTES = 62 * 2**20
PROJECT_BYTES = 24 * 2**20


def prep_kv_kernel(groups, place_ref, keys_ref, values_ref, gain_ref, *refs):
    out_refs, normed_ref = refs[:-1], refs[-1]
    wide = keys_ref[...].astype(jnp.float32)
    mean_square = jnp.mean(wide * wide, axis=-1, keepdims=True)
    normed_ref[...] = (wide * lax.rsqrt(mean_square + 1e-06) * gain_ref[...][None, :]).astype(jnp.bfloat16)
    share = wide.shape[1] // groups
    low, high = CHUNKS[0]
    for d, out_ref in zip(TURNS, out_refs):
        start = (place_ref[0] + d + groups) % groups * share + low * HS
        cols = pl.ds(pl.multiple_of(start, HS), (high - low) * HS)
        out_ref[0] = normed_ref[:, cols]
        out_ref[1] = values_ref[:, cols]
    low, high = CHUNKS[1]
    for dest in range(groups):
        cols = slice(dest * share + low * HS, dest * share + high * HS)
        out_refs[-1][dest, 0] = normed_ref[:, cols]
        out_refs[-1][dest, 1] = values_ref[:, cols]


def pack_kernel(core_ref, weight_ref, out_ref):
    out_ref[0] = weight_ref[...]


def pack(core, weight, groups):
    depth, width = weight.shape
    half = width // groups // 2
    return pl.pallas_call(
        pack_kernel,
        grid_spec=pltpu.PrefetchScalarGridSpec(
            num_scalar_prefetch=1,
            grid=(groups,),
            in_specs=[pl.BlockSpec((depth, half), lambda dest, core: (0, 2 * dest + core[0]))],
            out_specs=pl.BlockSpec((1, depth, half), lambda dest, core: (dest, 0, 0)),
        ),
        out_shape=jax.ShapeDtypeStruct((groups, depth, half), weight.dtype),
        name="pack",
    )(core, weight)


def prep_q_kernel(groups, queries_ref, gain_ref, out_ref):
    wide = queries_ref[...].astype(jnp.float32)
    mean_square = jnp.mean(wide * wide, axis=-1, keepdims=True)
    scaled_gain = gain_ref[...][None, :] * (LOG2E / HS**0.5)
    normed = (wide * lax.rsqrt(mean_square + 1e-06) * scaled_gain).astype(jnp.bfloat16)
    share = normed.shape[1] // groups
    for dest in range(groups):
        out_ref[dest] = normed[:, dest * share : (dest + 1) * share]


def attend_kernel(active_ref, q_ref, *refs):
    slots, (out_ref, acc_ref, max_ref) = refs[:WINDOW], refs[WINDOW:]
    length = out_ref.shape[0]
    ones = jnp.ones((length, HS), jnp.bfloat16)

    def key_of(index):
        return slots[index][:, 0].reshape(length, HS)

    def value_of(index):
        return jnp.concatenate([slots[index][:, 1].reshape(length, HS), ones], axis=1)

    def scores_of(query, index):
        return lax.dot_general(
            query, key_of(index), (((1,), (1,)), ((), ())), preferred_element_type=jnp.float32
        )

    def times_value(weights, index):
        return jnp.dot(
            weights.astype(jnp.bfloat16), value_of(index), preferred_element_type=jnp.float32
        )

    total = None
    for index in range(WINDOW):
        scores = scores_of(q_ref[...], index)
        if index:
            scores = scores + jnp.where(active_ref[index] != 0, 0.0, -1e30)
        part = times_value(jnp.exp2(scores), index)
        total = part if total is None else total + part
    acc_ref[...] = total
    denom = total[:, HS:]
    in_range = (jnp.min(denom) > NEAR) & (jnp.max(denom) < FAR)

    @pl.when(jnp.logical_not(in_range))
    def _():
        def redo(block, _):
            rows = pl.ds(pl.multiple_of(block * HS, HS), HS)
            query = q_ref[rows, :]
            for index in range(WINDOW):

                @pl.when(active_ref[index] != 0)
                def _():
                    scores = scores_of(query, index)
                    new_max = jnp.max(scores, axis=1, keepdims=True)
                    if index:
                        old_max = max_ref[...]
                        new_max = jnp.maximum(old_max, new_max)
                    part = times_value(jnp.exp2(scores - new_max), index)
                    if index:
                        part = acc_ref[rows, :] * jnp.exp2(old_max - new_max) + part
                    max_ref[...] = new_max
                    acc_ref[rows, :] = part

            return 0

        lax.fori_loop(0, length // HS, redo, 0)

    out_ref[...] = (acc_ref[:, :HS] / acc_ref[:, HS:]).astype(jnp.bfloat16)


def attend(active, query, slots, low, high):
    length, heads = query.shape[0], high - low
    groups, _, rows, _ = slots[0].shape
    grid_spec = pltpu.PrefetchScalarGridSpec(
        num_scalar_prefetch=1,
        grid=(heads,),
        in_specs=[pl.BlockSpec((length, HS), lambda head, _: (0, low + head))]
        + [pl.BlockSpec((groups, 2, rows, HS), lambda head, _: (0, 0, 0, head))] * WINDOW,
        out_specs=pl.BlockSpec((length, HS), lambda head, _: (0, head)),
        scratch_shapes=[
            pltpu.VMEM((length, 2 * HS), jnp.float32),
            pltpu.VMEM((HS, 1), jnp.float32),
        ],
    )
    flops = heads * WINDOW * length * length * HS * 8
    return pl.pallas_call(
        attend_kernel,
        grid_spec=grid_spec,
        out_shape=jax.ShapeDtypeStruct((length, heads * HS), jnp.bfloat16),
        compiler_params=pltpu.CompilerParams(vmem_limit_bytes=VMEM_BYTES),
        cost_estimate=pl.CostEstimate(
            flops=flops, bytes_accessed=20 * length * heads * HS * 2, transcendentals=0
        ),
        name="attend",
    )(active, query, *slots)


def part_copies(parts, held_ref, sems):
    depth = parts[0].shape[1]
    return [
        pltpu.make_async_copy(
            part, held_ref.at[:, pl.ds(index * depth, depth)], sems.at[index]
        )
        for index, part in enumerate(parts)
    ]


def weight_copies(place, weight_ref, span, held_ref, sems):
    count = len(TURNS)
    depth = (span[1] - span[0]) * HS
    return [
        pltpu.make_async_copy(
            weight_ref.at[(place - d + count) % count, pl.ds(span[0] * HS, depth), :],
            held_ref.at[pl.ds(index * depth, depth), :],
            sems.at[index],
        )
        for index, d in enumerate(TURNS)
    ]


def product(left, right):
    return jnp.dot(left[...], right[...], preferred_element_type=jnp.float32)


def project_early_kernel(span, place_ref, *refs):
    parts, refs = refs[: len(TURNS)], refs[len(TURNS) :]
    near_ref, far_ref, near_out, far_out, left, near_held, far_held, sems = refs
    first = part_copies(parts, left, sems.at[0])
    first += weight_copies(place_ref[0], near_ref, span, near_held, sems.at[1])
    second = weight_copies(place_ref[0], far_ref, span, far_held, sems.at[2])
    for copy in first + second:
        copy.start()
    for copy in first:
        copy.wait()
    near_out[...] = product(left, near_held)
    for copy in second:
        copy.wait()
    far_out[...] = product(left, far_held)


def project_early(place, parts, near, far, span):
    length, width = parts[0].shape[0], near.shape[2]
    depth = (span[1] - span[0]) * HS
    shape = jax.ShapeDtypeStruct((length, width), jnp.float32)
    smem = pl.BlockSpec(memory_space=pltpu.SMEM)
    return pl.pallas_call(
        functools.partial(project_early_kernel, span),
        in_specs=[smem] + [pl.BlockSpec(memory_space=pl.ANY)] * (len(parts) + 2),
        out_shape=(shape, shape),
        scratch_shapes=[
            pltpu.VMEM((length, len(TURNS) * depth), jnp.bfloat16),
            pltpu.VMEM((len(TURNS) * depth, width), jnp.bfloat16),
            pltpu.VMEM((len(TURNS) * depth, width), jnp.bfloat16),
            pltpu.SemaphoreType.DMA((3, len(TURNS))),
        ],
        compiler_params=pltpu.CompilerParams(vmem_limit_bytes=PROJECT_BYTES),
        cost_estimate=pl.CostEstimate(
            flops=2 * length * near.size, bytes_accessed=4 * near.size, transcendentals=0
        ),
        name="project_early",
    )(place, *parts, near, far)


def project_late_kernel(span, place_ref, gate_ref, early_ref, *refs):
    count = len(TURNS)
    parts, weight_ref = refs[:count], refs[count]
    out_refs, (whole_ref, left, held_ref, sems) = refs[count + 1 : -4], refs[-4:]
    copies = part_copies(parts, left, sems.at[0])
    copies += weight_copies(place_ref[0], weight_ref, span, held_ref, sems.at[1])
    for copy in copies:
        copy.start()
    for copy in copies:
        copy.wait()
    total = early_ref[...] + product(left, held_ref)
    whole_ref[...] = (total * gate_ref[...]).astype(jnp.bfloat16)
    rows = whole_ref.shape[0] // count
    for d, out_ref in zip(TURNS, out_refs):
        start = pl.multiple_of((place_ref[0] + d + count) % count * rows, rows)
        out_ref[...] = whole_ref[pl.ds(start, rows), :]


def project_late(place, gate_row, early, parts, weight, span):
    length, width = early.shape
    depth = (span[1] - span[0]) * HS
    smem, vmem = pl.BlockSpec(memory_space=pltpu.SMEM), pl.BlockSpec(memory_space=pltpu.VMEM)
    return pl.pallas_call(
        functools.partial(project_late_kernel, span),
        in_specs=[smem, vmem, vmem] + [pl.BlockSpec(memory_space=pl.ANY)] * (len(parts) + 1),
        out_shape=[jax.ShapeDtypeStruct((length // len(TURNS), width), jnp.bfloat16)] * len(TURNS),
        scratch_shapes=[
            pltpu.VMEM((length, width), jnp.bfloat16),
            pltpu.VMEM((length, len(TURNS) * depth), jnp.bfloat16),
            pltpu.VMEM((len(TURNS) * depth, width), jnp.bfloat16),
            pltpu.SemaphoreType.DMA((2, len(TURNS))),
        ],
        compiler_params=pltpu.CompilerParams(vmem_limit_bytes=PROJECT_BYTES),
        cost_estimate=pl.CostEstimate(
            flops=length * weight.size, bytes_accessed=2 * weight.size, transcendentals=0
        ),
        name="project_late",
    )(place, gate_row, early, *parts, weight)


def assemble_kernel(place_ref, core_ref, *refs):
    parts, out_ref = refs[:-1], refs[-1]
    count = len(TURNS)
    half = parts[0].shape[1]
    for index, part in enumerate(parts):
        source = (place_ref[0] - TURNS[index % count] + count) % count
        side = core_ref[0] if index < count else 1 - core_ref[0]
        start = pl.multiple_of((2 * source + side) * half, HS)
        out_ref[:, pl.ds(start, half)] = part[...]


def assemble(place, core, parts):
    rows, half = parts[0].shape
    smem, vmem = pl.BlockSpec(memory_space=pltpu.SMEM), pl.BlockSpec(memory_space=pltpu.VMEM)
    return pl.pallas_call(
        assemble_kernel,
        in_specs=[smem, smem] + [vmem] * len(parts),
        out_shape=jax.ShapeDtypeStruct((rows, half * len(parts)), jnp.bfloat16),
        name="assemble",
    )(place, core, *parts)


def shards(
    queries, keys, values, q_gain, k_gain, out_weight, gate_table, noise_level, first_stretch
):
    groups = lax.axis_size("seq")
    rows, feats = queries.shape
    share = feats // groups
    spot = lax.axis_index("stretch")
    place = lax.axis_index("seq")
    core, x_at = spot % 2, (spot // 2) % 4

    chips = lax.axis_size("stretch") // 2

    def chip_step(steps):
        return [
            (2 * chip + c, 2 * ((chip + steps) % chips) + c)
            for chip in range(chips)
            for c in range(2)
        ]

    def row_step(steps):
        return [
            (2 * chip + c, 2 * (chip // 4 * 4 + (chip + steps) % 4) + c)
            for chip in range(chips)
            for c in range(2)
        ]

    def along(value, pairs, label):
        with jax.named_scope(label):
            return lax.ppermute(value, "stretch", pairs)

    def swap(value, label):
        return along(value, [(i, i ^ 1) for i in range(2 * chips)], "swap_" + label)

    def turn(value, d, label):
        if not d:
            return value
        with jax.named_scope(f"{label}_turn_{d % groups}"):
            return lax.ppermute(value, "seq", [(i, (i + d) % groups) for i in range(groups)])


    place_word = place[None].astype(jnp.int32)
    core_word = core[None].astype(jnp.int32)
    sizes = [(high - low) * HS for low, high in CHUNKS]
    kv_shapes = [jax.ShapeDtypeStruct((2, rows, sizes[0]), jnp.bfloat16) for _ in TURNS] + [
        jax.ShapeDtypeStruct((groups, 2, rows, sizes[1]), jnp.bfloat16)
    ]
    smem, vmem = pl.BlockSpec(memory_space=pltpu.SMEM), pl.BlockSpec(memory_space=pltpu.VMEM)
    kv_pieces = pl.pallas_call(
        functools.partial(prep_kv_kernel, groups),
        in_specs=[smem, vmem, vmem, vmem],
        out_shape=kv_shapes,
        scratch_shapes=[pltpu.VMEM((rows, feats), jnp.bfloat16)],
        name="prep_kv",
    )(place_word, keys, values, k_gain)
    count = len(TURNS)
    width = out_weight.shape[1] // groups
    half = width // 2

    def after(done, *waiting):
        return lax.optimization_barrier((done, waiting))[1]

    def shift(own, c):
        return along(own, chip_step(4), f"shift{c}")

    def row_pair(own, shifted):
        return jnp.where(x_at < 3, own, shifted), jnp.where(x_at > 0, shifted, own)

    def core_pair(own, shifted):
        return jnp.where(core == 0, own, shifted)

    offsets = jnp.where(
        core == 0,
        jnp.array((0, 7, 2, 1, 6, 5, 4, 3), jnp.int32),
        jnp.array((0, 1, 2, 3, 6, 7, 4, 5), jnp.int32),
    )
    active = (offsets <= spot - first_stretch[0]).astype(jnp.int32)

    first_pieces = [turn(piece, d, "kv0") for piece, d in zip(kv_pieces[:count], TURNS)]
    q_parts = pl.pallas_call(
        functools.partial(prep_q_kernel, groups),
        out_shape=jax.ShapeDtypeStruct((groups, rows, share), jnp.bfloat16),
        name="prep_q",
    )(queries, q_gain)

    first_pieces, q_parts = after(q_parts, first_pieces, q_parts)
    own0 = jnp.stack(first_pieces)
    (rest,) = after(own0, kv_pieces[-1])
    packed = pack(core_word, out_weight, groups)
    own1 = lax.all_to_all(rest, "seq", 0, 0)
    shift0, packed, own1 = after((packed, own1), shift(own0, 0), packed, own1)

    right0, left0 = row_pair(own0, shift0)
    one0, three0 = along(right0, row_step(1), "one0"), along(left0, row_step(-1), "three0")
    pair0 = swap(core_pair(own0, shift0), "pair0")
    shift1 = shift(own1, 1)
    (q_parts,) = after(own1, q_parts)
    query = lax.all_to_all(q_parts, "seq", 0, 0).reshape(groups * rows, share)

    shift1, next_one0 = after((one0, three0, shift1, query), shift1, one0)
    two0 = along(next_one0, chip_step(1), "two0")
    right1, left1 = row_pair(own1, shift1)
    one1, three1 = along(right1, row_step(1), "one1"), along(left1, row_step(-1), "three1")
    one0s, three0s = swap(one0, "one0"), swap(three0, "three0")
    pair1 = swap(core_pair(own1, shift1), "pair1")
    (packed,) = after((query, pair1), packed)
    near = lax.all_to_all(packed, "seq", 0, 0)
    (next_two0,) = after(three1, two0)
    two1 = along(three1, chip_step(-1), "two1")
    three1s = swap(three1, "three1")
    two0s = swap(next_two0, "two0")
    (query,) = after((pair1, three1s), query)
    slots = (own0, pair0, one0, one0s, three0, three0s, two0, two0s)
    attended0 = attend(active, query, slots, *CHUNKS[0])
    gathered0 = [turn(attended0, d, "attended0") for d in TURNS]
    next_one1, next_two1 = after((attended0, one1, two1), one1, two1)
    one1s, two1s = swap(next_one1, "one1"), swap(next_two1, "two1")
    (near,) = after((one1s, two1s), near)
    far = swap(near, "weight")
    slots = (own1, pair1, one1, one1s, three1, three1s, two1, two1s)
    attended1 = attend(active, query, slots, *CHUNKS[1])
    gathered1 = [turn(attended1, d, "attended1") for d in TURNS]

    early_span, late_span = (0, CHUNKS[-1][0]), CHUNKS[-1]
    gate_row = lax.dynamic_slice(
        gate_table, (noise_level[0], place * width), (1, width)
    ).astype(jnp.float32)
    mixed = []
    for weight, early, side in zip(
        (near, far), project_early(place_word, gathered0, near, far, early_span), (core, 1 - core)
    ):
        gate_half = lax.dynamic_slice_in_dim(gate_row, side * half, half, 1)
        pieces = project_late(place_word, gate_half, early, gathered1, weight, late_span)
        mixed += [turn(piece, d, "mixed") for piece, d in zip(pieces, TURNS)]
    return assemble(place_word, core_word, mixed)


def solution(mesh):
    return jax.shard_map(
        shards,
        mesh=mesh,
        in_specs=(
            P(("stretch", "seq"), None),
            P(("stretch", "seq"), None),
            P(("stretch", "seq"), None),
            P(),
            P(),
            P("seq", None),
            P(),
            P("stretch"),
            P("stretch"),
        ),
        out_specs=P(("stretch", "seq"), None),
        check_vma=False,
    )
```

```python
import functools

import jax
import jax.numpy as jnp
from jax import lax
from jax.experimental import pallas as pl
from jax.experimental.pallas import tpu as pltpu
from jax.sharding import PartitionSpec as P

HS = 128
WINDOW = 8
LOG2E = 1.4426950408889634
CHUNKS = ((0, 2), (2, 5))
TURNS = (0, 1, -1, 2)
NEAR, FAR = 2.0**-60, 2.0**100
VMEM_BYTES = 62 * 2**20
PROJECT_BYTES = 24 * 2**20


def prep_kv_kernel(groups, place_ref, keys_ref, values_ref, gain_ref, *refs):
    out_refs, normed_ref = refs[:-1], refs[-1]
    wide = keys_ref[...].astype(jnp.float32)
    mean_square = jnp.mean(wide * wide, axis=-1, keepdims=True)
    normed_ref[...] = (wide * lax.rsqrt(mean_square + 1e-06) * gain_ref[...][None, :]).astype(jnp.bfloat16)
    share = wide.shape[1] // groups
    low, high = CHUNKS[0]
    for d, out_ref in zip(TURNS, out_refs):
        start = (place_ref[0] + d + groups) % groups * share + low * HS
        cols = pl.ds(pl.multiple_of(start, HS), (high - low) * HS)
        out_ref[0] = normed_ref[:, cols]
        out_ref[1] = values_ref[:, cols]
    low, high = CHUNKS[1]
    for dest in range(groups):
        cols = slice(dest * share + low * HS, dest * share + high * HS)
        out_refs[-1][dest, 0] = normed_ref[:, cols]
        out_refs[-1][dest, 1] = values_ref[:, cols]


def pack_kernel(core_ref, weight_ref, out_ref):
    out_ref[0] = weight_ref[...]


def pack(core, weight, groups):
    depth, width = weight.shape
    half = width // groups // 2
    return pl.pallas_call(
        pack_kernel,
        grid_spec=pltpu.PrefetchScalarGridSpec(
            num_scalar_prefetch=1,
            grid=(groups,),
            in_specs=[pl.BlockSpec((depth, half), lambda dest, core: (0, 2 * dest + core[0]))],
            out_specs=pl.BlockSpec((1, depth, half), lambda dest, core: (dest, 0, 0)),
        ),
        out_shape=jax.ShapeDtypeStruct((groups, depth, half), weight.dtype),
        name="pack",
    )(core, weight)


def prep_q_kernel(groups, queries_ref, gain_ref, out_ref):
    wide = queries_ref[...].astype(jnp.float32)
    mean_square = jnp.mean(wide * wide, axis=-1, keepdims=True)
    scaled_gain = gain_ref[...][None, :] * (LOG2E / HS**0.5)
    normed = (wide * lax.rsqrt(mean_square + 1e-06) * scaled_gain).astype(jnp.bfloat16)
    share = normed.shape[1] // groups
    for dest in range(groups):
        out_ref[dest] = normed[:, dest * share : (dest + 1) * share]


def attend_kernel(active_ref, q_ref, *refs):
    slots, (out_ref, acc_ref, max_ref) = refs[:WINDOW], refs[WINDOW:]
    length = out_ref.shape[0]
    ones = jnp.ones((length, HS), jnp.bfloat16)

    def key_of(index):
        return slots[index][:, 0].reshape(length, HS)

    def value_of(index):
        return jnp.concatenate([slots[index][:, 1].reshape(length, HS), ones], axis=1)

    def scores_of(query, index):
        return lax.dot_general(
            query, key_of(index), (((1,), (1,)), ((), ())), preferred_element_type=jnp.float32
        )

    def times_value(weights, index):
        return jnp.dot(
            weights.astype(jnp.bfloat16), value_of(index), preferred_element_type=jnp.float32
        )

    total = None
    for index in range(WINDOW):
        scores = scores_of(q_ref[...], index)
        if index:
            scores = scores + jnp.where(active_ref[index] != 0, 0.0, -1e30)
        part = times_value(jnp.exp2(scores), index)
        total = part if total is None else total + part
    acc_ref[...] = total
    denom = total[:, HS:]
    in_range = (jnp.min(denom) > NEAR) & (jnp.max(denom) < FAR)

    @pl.when(jnp.logical_not(in_range))
    def _():
        def redo(block, _):
            rows = pl.ds(pl.multiple_of(block * HS, HS), HS)
            query = q_ref[rows, :]
            for index in range(WINDOW):

                @pl.when(active_ref[index] != 0)
                def _():
                    scores = scores_of(query, index)
                    new_max = jnp.max(scores, axis=1, keepdims=True)
                    if index:
                        old_max = max_ref[...]
                        new_max = jnp.maximum(old_max, new_max)
                    part = times_value(jnp.exp2(scores - new_max), index)
                    if index:
                        part = acc_ref[rows, :] * jnp.exp2(old_max - new_max) + part
                    max_ref[...] = new_max
                    acc_ref[rows, :] = part

            return 0

        lax.fori_loop(0, length // HS, redo, 0)

    out_ref[...] = (acc_ref[:, :HS] / acc_ref[:, HS:]).astype(jnp.bfloat16)


def attend(active, query, slots, low, high):
    length, heads = query.shape[0], high - low
    groups, _, rows, _ = slots[0].shape
    grid_spec = pltpu.PrefetchScalarGridSpec(
        num_scalar_prefetch=1,
        grid=(heads,),
        in_specs=[pl.BlockSpec((length, HS), lambda head, _: (0, low + head))]
        + [pl.BlockSpec((groups, 2, rows, HS), lambda head, _: (0, 0, 0, head))] * WINDOW,
        out_specs=pl.BlockSpec((length, HS), lambda head, _: (0, head)),
        scratch_shapes=[
            pltpu.VMEM((length, 2 * HS), jnp.float32),
            pltpu.VMEM((HS, 1), jnp.float32),
        ],
    )
    flops = heads * WINDOW * length * length * HS * 8
    return pl.pallas_call(
        attend_kernel,
        grid_spec=grid_spec,
        out_shape=jax.ShapeDtypeStruct((length, heads * HS), jnp.bfloat16),
        compiler_params=pltpu.CompilerParams(vmem_limit_bytes=VMEM_BYTES),
        cost_estimate=pl.CostEstimate(
            flops=flops, bytes_accessed=20 * length * heads * HS * 2, transcendentals=0
        ),
        name="attend",
    )(active, query, *slots)


def part_copies(parts, held_ref, sems):
    depth = parts[0].shape[1]
    return [
        pltpu.make_async_copy(
            part, held_ref.at[:, pl.ds(index * depth, depth)], sems.at[index]
        )
        for index, part in enumerate(parts)
    ]


def weight_copies(place, weight_ref, span, held_ref, sems):
    count = len(TURNS)
    depth = (span[1] - span[0]) * HS
    return [
        pltpu.make_async_copy(
            weight_ref.at[(place - d + count) % count, pl.ds(span[0] * HS, depth), :],
            held_ref.at[pl.ds(index * depth, depth), :],
            sems.at[index],
        )
        for index, d in enumerate(TURNS)
    ]


def product(left, right):
    return jnp.dot(left[...], right[...], preferred_element_type=jnp.float32)


def project_early_kernel(span, place_ref, *refs):
    parts, refs = refs[: len(TURNS)], refs[len(TURNS) :]
    near_ref, far_ref, near_out, far_out, left, near_held, far_held, sems = refs
    first = part_copies(parts, left, sems.at[0])
    first += weight_copies(place_ref[0], near_ref, span, near_held, sems.at[1])
    second = weight_copies(place_ref[0], far_ref, span, far_held, sems.at[2])
    for copy in first + second:
        copy.start()
    for copy in first:
        copy.wait()
    near_out[...] = product(left, near_held)
    for copy in second:
        copy.wait()
    far_out[...] = product(left, far_held)


def project_early(place, parts, near, far, span):
    length, width = parts[0].shape[0], near.shape[2]
    depth = (span[1] - span[0]) * HS
    shape = jax.ShapeDtypeStruct((length, width), jnp.float32)
    smem = pl.BlockSpec(memory_space=pltpu.SMEM)
    return pl.pallas_call(
        functools.partial(project_early_kernel, span),
        in_specs=[smem] + [pl.BlockSpec(memory_space=pl.ANY)] * (len(parts) + 2),
        out_shape=(shape, shape),
        scratch_shapes=[
            pltpu.VMEM((length, len(TURNS) * depth), jnp.bfloat16),
            pltpu.VMEM((len(TURNS) * depth, width), jnp.bfloat16),
            pltpu.VMEM((len(TURNS) * depth, width), jnp.bfloat16),
            pltpu.SemaphoreType.DMA((3, len(TURNS))),
        ],
        compiler_params=pltpu.CompilerParams(vmem_limit_bytes=PROJECT_BYTES),
        cost_estimate=pl.CostEstimate(
            flops=2 * length * near.size, bytes_accessed=4 * near.size, transcendentals=0
        ),
        name="project_early",
    )(place, *parts, near, far)


def project_late_kernel(span, place_ref, gate_ref, early_ref, *refs):
    count = len(TURNS)
    parts, weight_ref = refs[:count], refs[count]
    out_refs, (whole_ref, left, held_ref, sems) = refs[count + 1 : -4], refs[-4:]
    copies = part_copies(parts, left, sems.at[0])
    copies += weight_copies(place_ref[0], weight_ref, span, held_ref, sems.at[1])
    for copy in copies:
        copy.start()
    for copy in copies:
        copy.wait()
    total = early_ref[...] + product(left, held_ref)
    whole_ref[...] = (total * gate_ref[...]).astype(jnp.bfloat16)
    rows = whole_ref.shape[0] // count
    for d, out_ref in zip(TURNS, out_refs):
        start = pl.multiple_of((place_ref[0] + d + count) % count * rows, rows)
        out_ref[...] = whole_ref[pl.ds(start, rows), :]


def project_late(place, gate_row, early, parts, weight, span):
    length, width = early.shape
    depth = (span[1] - span[0]) * HS
    smem, vmem = pl.BlockSpec(memory_space=pltpu.SMEM), pl.BlockSpec(memory_space=pltpu.VMEM)
    return pl.pallas_call(
        functools.partial(project_late_kernel, span),
        in_specs=[smem, vmem, vmem] + [pl.BlockSpec(memory_space=pl.ANY)] * (len(parts) + 1),
        out_shape=[jax.ShapeDtypeStruct((length // len(TURNS), width), jnp.bfloat16)] * len(TURNS),
        scratch_shapes=[
            pltpu.VMEM((length, width), jnp.bfloat16),
            pltpu.VMEM((length, len(TURNS) * depth), jnp.bfloat16),
            pltpu.VMEM((len(TURNS) * depth, width), jnp.bfloat16),
            pltpu.SemaphoreType.DMA((2, len(TURNS))),
        ],
        compiler_params=pltpu.CompilerParams(vmem_limit_bytes=PROJECT_BYTES),
        cost_estimate=pl.CostEstimate(
            flops=length * weight.size, bytes_accessed=2 * weight.size, transcendentals=0
        ),
        name="project_late",
    )(place, gate_row, early, *parts, weight)


def assemble_kernel(place_ref, core_ref, *refs):
    parts, out_ref = refs[:-1], refs[-1]
    count = len(TURNS)
    half = parts[0].shape[1]
    for index, part in enumerate(parts):
        source = (place_ref[0] - TURNS[index % count] + count) % count
        side = core_ref[0] if index < count else 1 - core_ref[0]
        start = pl.multiple_of((2 * source + side) * half, HS)
        out_ref[:, pl.ds(start, half)] = part[...]


def assemble(place, core, parts):
    rows, half = parts[0].shape
    smem, vmem = pl.BlockSpec(memory_space=pltpu.SMEM), pl.BlockSpec(memory_space=pltpu.VMEM)
    return pl.pallas_call(
        assemble_kernel,
        in_specs=[smem, smem] + [vmem] * len(parts),
        out_shape=jax.ShapeDtypeStruct((rows, half * len(parts)), jnp.bfloat16),
        name="assemble",
    )(place, core, *parts)


def shards(
    queries, keys, values, q_gain, k_gain, out_weight, gate_table, noise_level, first_stretch
):
    groups = lax.axis_size("seq")
    rows, feats = queries.shape
    share = feats // groups
    spot = lax.axis_index("stretch")
    place = lax.axis_index("seq")
    core, x_at = spot % 2, (spot // 2) % 4

    chips = lax.axis_size("stretch") // 2

    def chip_step(steps):
        return [
            (2 * chip + c, 2 * ((chip + steps) % chips) + c)
            for chip in range(chips)
            for c in range(2)
        ]

    def row_step(steps):
        return [
            (2 * chip + c, 2 * (chip // 4 * 4 + (chip + steps) % 4) + c)
            for chip in range(chips)
            for c in range(2)
        ]

    def along(value, pairs, label):
        with jax.named_scope(label):
            return lax.ppermute(value, "stretch", pairs)

    def swap(value, label):
        return along(value, [(i, i ^ 1) for i in range(2 * chips)], "swap_" + label)

    def turn(value, d, label):
        if not d:
            return value
        with jax.named_scope(f"{label}_turn_{d % groups}"):
            return lax.ppermute(value, "seq", [(i, (i + d) % groups) for i in range(groups)])


    place_word = place[None].astype(jnp.int32)
    core_word = core[None].astype(jnp.int32)
    sizes = [(high - low) * HS for low, high in CHUNKS]
    kv_shapes = [jax.ShapeDtypeStruct((2, rows, sizes[0]), jnp.bfloat16) for _ in TURNS] + [
        jax.ShapeDtypeStruct((groups, 2, rows, sizes[1]), jnp.bfloat16)
    ]
    smem, vmem = pl.BlockSpec(memory_space=pltpu.SMEM), pl.BlockSpec(memory_space=pltpu.VMEM)
    kv_pieces = pl.pallas_call(
        functools.partial(prep_kv_kernel, groups),
        in_specs=[smem, vmem, vmem, vmem],
        out_shape=kv_shapes,
        scratch_shapes=[pltpu.VMEM((rows, feats), jnp.bfloat16)],
        name="prep_kv",
    )(place_word, keys, values, k_gain)
    count = len(TURNS)
    width = out_weight.shape[1] // groups
    half = width // 2

    def after(done, *waiting):
        return lax.optimization_barrier((done, waiting))[1]

    def shift(own, c):
        return along(own, chip_step(4), f"shift{c}")

    def row_pair(own, shifted):
        return jnp.where(x_at < 3, own, shifted), jnp.where(x_at > 0, shifted, own)

    def core_pair(own, shifted):
        return jnp.where(core == 0, own, shifted)

    offsets = jnp.where(
        core == 0,
        jnp.array((0, 7, 2, 1, 6, 5, 4, 3), jnp.int32),
        jnp.array((0, 1, 2, 3, 6, 7, 4, 5), jnp.int32),
    )
    active = (offsets <= spot - first_stretch[0]).astype(jnp.int32)

    first_pieces = [turn(piece, d, "kv0") for piece, d in zip(kv_pieces[:count], TURNS)]
    q_parts = pl.pallas_call(
        functools.partial(prep_q_kernel, groups),
        out_shape=jax.ShapeDtypeStruct((groups, rows, share), jnp.bfloat16),
        name="prep_q",
    )(queries, q_gain)

    first_pieces, q_parts = after(q_parts, first_pieces, q_parts)
    own0 = jnp.stack(first_pieces)
    (rest,) = after(own0, kv_pieces[-1])
    packed = pack(core_word, out_weight, groups)
    own1 = lax.all_to_all(rest, "seq", 0, 0)
    shift0, packed, own1 = after((packed, own1), shift(own0, 0), packed, own1)

    right0, left0 = row_pair(own0, shift0)
    one0, three0 = along(right0, row_step(1), "one0"), along(left0, row_step(-1), "three0")
    pair0 = swap(core_pair(own0, shift0), "pair0")
    shift1 = shift(own1, 1)
    (q_parts,) = after(own1, q_parts)
    query = lax.all_to_all(q_parts, "seq", 0, 0).reshape(groups * rows, share)

    shift1, next_one0 = after((one0, three0, shift1, query), shift1, one0)
    two0 = along(next_one0, chip_step(1), "two0")
    right1, left1 = row_pair(own1, shift1)
    one1, three1 = along(right1, row_step(1), "one1"), along(left1, row_step(-1), "three1")
    one0s, three0s = swap(one0, "one0"), swap(three0, "three0")
    pair1 = swap(core_pair(own1, shift1), "pair1")
    (packed,) = after((query, pair1), packed)
    near = lax.all_to_all(packed, "seq", 0, 0)
    (next_two0,) = after(three1, two0)
    two1 = along(three1, chip_step(-1), "two1")
    three1s = swap(three1, "three1")
    two0s = swap(next_two0, "two0")
    (query,) = after((pair1, three1s), query)
    slots = (own0, pair0, one0, one0s, three0, three0s, two0, two0s)
    attended0 = attend(active, query, slots, *CHUNKS[0])
    gathered0 = [turn(attended0, d, "attended0") for d in TURNS]
    next_one1, next_two1 = after((attended0, one1, two1), one1, two1)
    one1s, two1s = swap(next_one1, "one1"), swap(next_two1, "two1")
    (near,) = after((one1s, two1s), near)
    far = swap(near, "weight")
    slots = (own1, pair1, one1, one1s, three1, three1s, two1, two1s)
    attended1 = attend(active, query, slots, *CHUNKS[1])
    gathered1 = [turn(attended1, d, "attended1") for d in TURNS]

    early_span, late_span = (0, CHUNKS[-1][0]), CHUNKS[-1]
    gate_row = lax.dynamic_slice(
        gate_table, (noise_level[0], place * width), (1, width)
    ).astype(jnp.float32)
    mixed = []
    for weight, early, side in zip(
        (near, far), project_early(place_word, gathered0, near, far, early_span), (core, 1 - core)
    ):
        gate_half = lax.dynamic_slice_in_dim(gate_row, side * half, half, 1)
        pieces = project_late(place_word, gate_half, early, gathered1, weight, late_span)
        mixed += [turn(piece, d, "mixed") for piece, d in zip(pieces, TURNS)]
    return assemble(place_word, core_word, mixed)


def solution(mesh):
    return jax.shard_map(
        shards,
        mesh=mesh,
        in_specs=(
            P(("stretch", "seq"), None),
            P(("stretch", "seq"), None),
            P(("stretch", "seq"), None),
            P(),
            P(),
            P("seq", None),
            P(),
            P("stretch"),
            P("stretch"),
        ),
        out_specs=P(("stretch", "seq"), None),
        check_vma=False,
    )
```
